32 devices in a mesh: wide: 8 (over y, x, core), rep: 4 (over z).
Axes of the slice: x: 2, y: 2, z: 4, core: 2. Of those that a mesh axis runs over, the one named last changes fastest.
Arguments:
- passages: bfloat16 [32768, 1024], P(('wide', 'rep')), may hold values from -6 to 6
- cluster_ids: int32 [32768], P(('wide', 'rep')), may hold values from 0 to 131071, as said below
- w_first: bfloat16 [1024, 1024], replicated, may hold values from -0.1875 to 0.1875
- w_second: bfloat16 [1024, 256], replicated, may hold values from -0.1875 to 0.1875
- centroids: bfloat16 [131072, 256], P('wide'), may hold values from -6 to 6
Outputs:
- refreshed: bfloat16 [131072, 256], P(('wide', 'rep'))
- residuals: bfloat16 [32768, 256], P(('wide', 'rep'))
The draws below stay inside these ranges and needn't reach their ends.
Inputs may be any that keep to these rules, and one draw needn't show every extreme that they name: The owner of a passage is cluster_ids // 16384. Among the 1024 rows of one device (aligned blocks), at most 384 have any one owner; in every draw one owner gets exactly 384 rows from every device's block.
All inputs are finite; a program needn't handle non-finite values.
Results may differ from the reference program's by a relative error of at most 0.015.
Values may be sent and summed in bfloat16 or wider, within the bound.
A program may use at most 128 MiB of HBM per device.

```python
import jax
import jax.numpy as jnp
from jax import lax

D = 1024
E = 256
CENT_DEV = 16384
TOK_DEV = 1024
CAP = 384
CLUSTERS = 131072
TOKENS = 32768
N_REP = 4


def draw_cluster_ids(key, part):
    owner_count = CLUSTERS // CENT_DEV
    device_count = TOKENS // TOK_DEV
    hot_key, dev_key = jax.random.split(jax.random.fold_in(key, 11))
    hot_owner = jax.random.randint(hot_key, (), 0, owner_count)

    def one_device(dkey):
        order_key, offset_key, local_key = jax.random.split(dkey, 3)
        row_ranks = jax.random.permutation(order_key, TOK_DEV).astype(jnp.int32)
        offset_by = jax.random.randint(offset_key, (), 0, owner_count - 1)
        others = (row_ranks - CAP + offset_by) % (owner_count - 1)
        others = others + (others >= hot_owner).astype(jnp.int32)
        owner_ids = jnp.where(row_ranks < CAP, hot_owner, others)
        local_ids = jax.random.randint(local_key, (TOK_DEV,), 0, CENT_DEV)
        return owner_ids * CENT_DEV + local_ids
    device_keys = jax.random.split(dev_key, device_count)
    return jax.vmap(one_device)(device_keys).reshape(TOKENS).astype(jnp.int32)


def block_scale(key, extent, shards, least, high):
    def one(dim, parts):
        heights = jax.random.uniform(jax.random.fold_in(jax.random.fold_in(key, 6), dim), (parts,), jnp.float32, least / len(shards), high / len(shards))
        return jnp.repeat(jnp.exp(heights), extent[dim] // parts).reshape((-1,) + (1,) * (len(extent) - dim - 1))

    loudness = one(*shards[0])
    for cut in shards[1:]:
        loudness = loudness * one(*cut)
    return loudness


def gaussian(rng, shape, spread, bound, shards=(), held_as=jnp.bfloat16):
    factor_of = block_scale(rng, shape, shards, -0.22, 0.18) if shards else 1.0
    entries = jax.random.normal(rng, shape, jnp.float32) * spread * factor_of
    return jnp.minimum(jnp.maximum(entries, -bound), bound).astype(held_as)


def setup_inputs(seed: int = 0) -> dict:
    key_of = jax.random.split(jax.random.key(seed), 6)
    passages = gaussian(key_of[0], (TOKENS, D), 1.0, 6.0, ((0, 32),))
    cluster_ids = draw_cluster_ids(jax.random.fold_in(key_of[5], 71), 0)
    w_first = gaussian(key_of[2], (D, D), D ** -0.5, 0.1875)
    w_second = gaussian(key_of[3], (D, E), D ** -0.5, 0.1875)
    centroids = gaussian(key_of[4], (CLUSTERS, E), 1.0, 6.0, ((0, 8),))
    return {"passages": passages, "cluster_ids": cluster_ids, "w_first": w_first, "w_second": w_second, "centroids": centroids}


def encode(row_block, w_first, w_second):
    hidden = jax.nn.gelu(jnp.dot(row_block, w_first, preferred_element_type=jnp.float32), approximate=True).astype(jnp.bfloat16)
    projected = jnp.dot(hidden, w_second, preferred_element_type=jnp.float32)
    scaled = projected * lax.rsqrt(lax.optimization_barrier(jnp.mean(projected * projected, axis=-1, keepdims=True)) + 1e-06)
    return scaled.astype(jnp.bfloat16)

def reference(passages, cluster_ids, w_first, w_second, centroids):
    blocks = passages.reshape(TOKENS // TOK_DEV, TOK_DEV, D)
    embedded = lax.map(lambda row_block: encode(row_block, w_first, w_second), blocks).reshape(TOKENS, E)
    values = embedded.astype(jnp.float32)
    replica_of = jnp.arange(TOKENS, dtype=jnp.int32) // TOK_DEV % N_REP
    summed = jnp.zeros((CLUSTERS, E), jnp.float32)
    for replica in range(N_REP):
        chosen = jnp.where((replica_of == replica)[:, None], values, jnp.float32(0.0))
        partial_value = jnp.zeros((CLUSTERS, E), jnp.float32).at[cluster_ids].add(chosen)
        rounded = lax.optimization_barrier(partial_value.astype(jnp.bfloat16))
        summed = summed + rounded.astype(jnp.float32)
    updated = centroids.astype(jnp.float32) + summed
    refreshed = (updated * lax.rsqrt(lax.optimization_barrier(jnp.mean(updated * updated, axis=-1, keepdims=True)) + 1e-06)).astype(jnp.bfloat16)
    residuals = (values - refreshed[cluster_ids].astype(jnp.float32)).astype(jnp.bfloat16)
    return (refreshed, residuals)
```

```python
import functools

import jax
import jax.numpy as jnp
from jax import lax
from jax.experimental import pallas as pl
from jax.experimental.pallas import tpu as pltpu
from jax.sharding import PartitionSpec as P

CHUNK = 128
GROUP = 8
EPS = 1e-06


def normalised(values):
    return values * lax.rsqrt(jnp.mean(values * values, axis=-1, keepdims=True) + EPS)


def sums_kernel(
    scalars, first, last, emb, ids, cent, own_ids, own_cent, own_emb, order,
    out_table, out_res, chunks, slots, acc, cent_buf, tile_res, sems, cent_sem,
    *, blocks, per_block, tile, row_block,
):
    n_chunks = blocks * per_block
    share = out_table.shape[0]
    tok = own_ids.shape[0]
    wide = GROUP * CHUNK

    cent_copy = pltpu.make_async_copy(
        cent.at[pl.ds(pl.multiple_of(scalars[1], 16), share)], cent_buf, cent_sem
    )
    cent_copy.start()

    def build(job):
        def block(k, count):
            begin = first[job * blocks + k]
            end = last[job * blocks + k]
            lo = begin // CHUNK
            hi = jnp.where(end > begin, (end + CHUNK - 1) // CHUNK, lo)

            def put(c, n):
                chunks[n] = k * per_block + c
                return n + 1

            return lax.fori_loop(lo, hi, put, count)

        count = lax.fori_loop(0, blocks, block, 0)
        for extra in range(GROUP):
            chunks[count + extra] = n_chunks
        return (count + GROUP - 1) // GROUP

    def copies(group, slot):
        made = []
        for j in range(GROUP):
            at = jnp.minimum(chunks[group * GROUP + j], n_chunks - 1)
            made.append(
                pltpu.make_async_copy(
                    emb.at[pl.ds(pl.multiple_of(at * CHUNK, CHUNK), CHUNK)],
                    slots.at[slot, pl.ds(j * CHUNK, CHUNK)],
                    sems.at[slot, j],
                )
            )
        return made

    def run(groups, step):
        @pl.when(groups > 0)
        def _():
            for copy in copies(0, 0):
                copy.start()

        def body(group, carry):
            slot = lax.rem(group, 2)

            @pl.when(group + 1 < groups)
            def _():
                for copy in copies(group + 1, 1 - slot):
                    copy.start()

            for copy in copies(group, slot):
                copy.wait()
            row = [ids[pl.ds(chunks[group * GROUP + j], 1), :] for j in range(GROUP)]
            step(jnp.concatenate(row, axis=1), slot)
            return carry

        lax.fori_loop(0, groups, body, 0)

    acc[...] = jnp.zeros_like(acc)
    groups = build(0)

    def table_step(id_row, slot):
        def rows(m, carry):
            at = pl.multiple_of(m * row_block, row_block)
            wanted = scalars[0] + at + lax.broadcasted_iota(jnp.int32, (row_block, wide), 0)
            pick = (wanted == id_row).astype(jnp.float32).astype(jnp.bfloat16)
            acc[pl.ds(at, row_block), :] += jnp.dot(
                pick, slots[slot], preferred_element_type=jnp.float32
            )
            return carry

        lax.fori_loop(0, share // row_block, rows, 0)

    run(groups, table_step)
    cent_copy.wait()

    def finish(m, carry):
        at = pl.ds(pl.multiple_of(m * row_block, row_block), row_block)
        updated = cent_buf[at, :].astype(jnp.float32) + acc[at, :]
        out_table[at, :] = normalised(updated).astype(jnp.bfloat16)
        return carry

    lax.fori_loop(0, share // row_block, finish, 0)

    def one_tile(i, carry):
        at = pl.ds(pl.multiple_of(i * tile, tile), tile)
        part = acc.at[pl.ds(0, tile)]
        part[...] = jnp.zeros((tile, acc.shape[1]), jnp.float32)
        groups = build(i + 1)

        def tile_step(id_row, slot):
            pick = (own_ids[at, :] == id_row).astype(jnp.float32).astype(jnp.bfloat16)
            part[...] += jnp.dot(pick, slots[slot], preferred_element_type=jnp.float32)

        run(groups, tile_step)
        fresh = normalised(own_cent[at, :].astype(jnp.float32) + part[...]).astype(jnp.bfloat16)
        tile_res[at, :] = (own_emb[at, :].astype(jnp.float32) - fresh.astype(jnp.float32)).astype(
            jnp.bfloat16
        )
        return carry

    lax.fori_loop(0, tok // tile, one_tile, 0)

    def unsort(i, carry):
        at = pl.multiple_of(i * tile, tile)
        wanted = at + lax.broadcasted_iota(jnp.int32, (tile, tok), 0)
        pick = (wanted == order[...]).astype(jnp.float32).astype(jnp.bfloat16)
        out_res[pl.ds(at, tile), :] = jnp.dot(
            pick, tile_res[...], preferred_element_type=jnp.float32
        ).astype(jnp.bfloat16)
        return carry

    lax.fori_loop(0, tok // tile, unsort, 0)


def body(passages, cluster_ids, w_first, w_second, centroids):
    tok = passages.shape[0]
    owners = lax.axis_size("wide")
    reps = lax.axis_size("rep")
    blocks = owners * reps
    cent_rows, emb_width = centroids.shape
    share = cent_rows // reps
    capacity = 3 * tok // owners
    per_block = tok // CHUNK
    tile = min(256, tok)
    tiles = tok // tile
    wide_at = lax.axis_index("wide")
    rep_at = lax.axis_index("rep")

    sorted_ids, order = lax.sort((cluster_ids, lax.iota(jnp.int32, tok)), num_keys=1)
    all_ids = lax.all_gather(sorted_ids, ("wide", "rep"), axis=0, tiled=False)

    hidden = jax.nn.gelu(
        jnp.dot(passages, w_first, preferred_element_type=jnp.float32), approximate=True
    ).astype(jnp.bfloat16)
    projected = jnp.dot(hidden, w_second, preferred_element_type=jnp.float32)
    embedded = normalised(projected).astype(jnp.bfloat16)
    to_sorted = (order[:, None] == jnp.arange(tok, dtype=jnp.int32)[None, :]).astype(jnp.bfloat16)
    own_emb = jnp.dot(to_sorted, embedded, preferred_element_type=jnp.float32).astype(jnp.bfloat16)
    all_emb = lax.all_gather(own_emb, ("wide", "rep"), axis=0, tiled=True)

    mine = lax.dynamic_index_in_dim(all_ids.reshape(owners, reps, tok), rep_at, 1, keepdims=False)
    owner_base = wide_at * cent_rows
    begin = jnp.sum((mine < owner_base).astype(jnp.int32), axis=1)
    padded = jnp.pad(mine, ((0, 0), (0, capacity)))
    asked = jnp.stack(
        [lax.dynamic_slice(padded[k], (begin[k],), (capacity,)) for k in range(owners)]
    )
    local = jnp.clip(asked - owner_base, 0, cent_rows - 1).reshape(owners * capacity)
    picked = centroids[local]
    returned = lax.all_to_all(picked, "wide", split_axis=0, concat_axis=0, tiled=True)
    owner_of = sorted_ids // cent_rows
    starts = jnp.sum(
        (sorted_ids[None, :] < jnp.arange(owners, dtype=jnp.int32)[:, None] * cent_rows).astype(
            jnp.int32
        ),
        axis=1,
    )
    member = (owner_of[:, None] == jnp.arange(owners, dtype=jnp.int32)[None, :]).astype(jnp.int32)
    place = owner_of * capacity + lax.iota(jnp.int32, tok) - jnp.sum(member * starts[None, :], axis=1)
    own_cent = returned[place]

    share_base = owner_base + rep_at * share
    lows = jnp.concatenate([share_base[None], sorted_ids[::tile]])
    highs = jnp.concatenate([share_base[None] + share, sorted_ids[tile - 1 :: tile] + 1])
    first = jnp.sum((all_ids[None] < lows[:, None, None]).astype(jnp.int32), axis=2).reshape(-1)
    last = jnp.sum((all_ids[None] < highs[:, None, None]).astype(jnp.int32), axis=2).reshape(-1)
    scalars = jnp.stack([share_base, rep_at * share])
    id_rows = jnp.concatenate(
        [all_ids.reshape(blocks * per_block, CHUNK), jnp.full((8, CHUNK), -1, jnp.int32)]
    )

    smem = pl.BlockSpec(memory_space=pltpu.SMEM)
    vmem = pl.BlockSpec(memory_space=pltpu.VMEM)
    hbm = pl.BlockSpec(memory_space=pl.ANY)
    return pl.pallas_call(
        functools.partial(
            sums_kernel, blocks=blocks, per_block=per_block, tile=tile, row_block=min(512, share)
        ),
        out_shape=(
            jax.ShapeDtypeStruct((share, emb_width), jnp.bfloat16),
            jax.ShapeDtypeStruct((tok, emb_width), jnp.bfloat16),
        ),
        in_specs=[smem, smem, smem, hbm, vmem, hbm, vmem, vmem, vmem, vmem],
        out_specs=(vmem, vmem),
        scratch_shapes=[
            pltpu.SMEM((blocks * per_block + GROUP,), jnp.int32),
            pltpu.VMEM((2, GROUP * CHUNK, emb_width), jnp.bfloat16),
            pltpu.VMEM((share, emb_width), jnp.float32),
            pltpu.VMEM((share, emb_width), jnp.bfloat16),
            pltpu.VMEM((tok, emb_width), jnp.bfloat16),
            pltpu.SemaphoreType.DMA((2, GROUP)),
            pltpu.SemaphoreType.DMA,
        ],
        compiler_params=pltpu.CompilerParams(vmem_limit_bytes=48 * 1024 * 1024),
        cost_estimate=pl.CostEstimate(
            flops=30_000_000_000, bytes_accessed=40_000_000, transcendentals=0
        ),
    )(
        scalars, first, last, all_emb, id_rows, centroids, sorted_ids[:, None], own_cent, own_emb,
        order[None, :],
    )


def solution(mesh):
    return jax.shard_map(
        body,
        mesh=mesh,
        in_specs=(P(("wide", "rep"), None), P(("wide", "rep")), P(), P(), P("wide", None)),
        out_specs=(P(("wide", "rep"), None), P(("wide", "rep"), None)),
        check_vma=False,
    )
```

```python
import functools

import jax
import jax.numpy as jnp
from jax import lax
from jax.experimental import pallas as pl
from jax.experimental.pallas import tpu as pltpu
from jax.sharding import PartitionSpec as P

CHUNK = 128
GROUP = 8
EPS = 1e-06
WIDE = ("chip", "core")


def normalised(values):
    return values * lax.rsqrt(jnp.mean(values * values, axis=-1, keepdims=True) + EPS)


def sums_kernel(
    scalars, first, last, emb, ids, cent, own_ids, own_cent, own_emb, order,
    out_table, out_res, chunks, slots, acc, cent_buf, tile_res, sems, cent_sem,
    *, blocks, per_block, stride, tile, row_block, resident,
):
    n_chunks = blocks * per_block
    share = out_table.shape[0]
    tok = own_ids.shape[0]
    wide = GROUP * CHUNK

    cent_copy = pltpu.make_async_copy(
        cent.at[pl.ds(pl.multiple_of(scalars[1], 16), share)], cent_buf, cent_sem
    )
    cent_copy.start()

    def row_of(n):
        return pl.multiple_of(lax.div(n, per_block) * stride + lax.rem(n, per_block) * CHUNK, 16)

    def whole_copies():
        rows = emb.shape[0] // GROUP
        return [
            pltpu.make_async_copy(
                emb.at[pl.ds(j * rows, rows)], slots.at[pl.ds(j * rows, rows)], sems.at[0, j]
            )
            for j in range(GROUP)
        ]

    if resident:
        for copy in whole_copies():
            copy.start()

    def build(job):
        def block(k, count):
            begin = first[job * blocks + k]
            end = last[job * blocks + k]
            lo = begin // CHUNK
            hi = jnp.where(end > begin, (end + CHUNK - 1) // CHUNK, lo)

            def put(c, n):
                chunks[n] = k * per_block + c
                return n + 1

            return lax.fori_loop(lo, hi, put, count)

        count = lax.fori_loop(0, blocks, block, 0)
        for extra in range(GROUP):
            chunks[count + extra] = n_chunks
        return (count + GROUP - 1) // GROUP

    def copies(group, slot):
        made = []
        for j in range(GROUP):
            at = jnp.minimum(chunks[group * GROUP + j], n_chunks - 1)
            made.append(
                pltpu.make_async_copy(
                    emb.at[pl.ds(row_of(at), CHUNK)],
                    slots.at[slot, pl.ds(j * CHUNK, CHUNK)],
                    sems.at[slot, j],
                )
            )
        return made

    def id_row_of(group):
        row = [ids[pl.ds(chunks[group * GROUP + j], 1), :] for j in range(GROUP)]
        return jnp.concatenate(row, axis=1)

    def run_resident(groups, step):
        def body(group, carry):
            at = [jnp.minimum(chunks[group * GROUP + j], n_chunks - 1) for j in range(GROUP)]
            rows = jnp.concatenate([slots[pl.ds(row_of(n), CHUNK), :] for n in at], axis=0)
            step(id_row_of(group), rows)
            return carry

        lax.fori_loop(0, groups, body, 0)

    def run_streamed(groups, step):
        @pl.when(groups > 0)
        def _():
            for copy in copies(0, 0):
                copy.start()

        def body(group, carry):
            slot = lax.rem(group, 2)

            @pl.when(group + 1 < groups)
            def _():
                for copy in copies(group + 1, 1 - slot):
                    copy.start()

            for copy in copies(group, slot):
                copy.wait()
            step(id_row_of(group), slots[slot])
            return carry

        lax.fori_loop(0, groups, body, 0)

    run = run_resident if resident else run_streamed

    acc[...] = jnp.zeros_like(acc)
    groups = build(0)
    if resident:
        for copy in whole_copies():
            copy.wait()

    def table_step(id_row, values):
        def rows(m, carry):
            at = pl.multiple_of(m * row_block, row_block)
            wanted = scalars[0] + at + lax.broadcasted_iota(jnp.int32, (row_block, wide), 0)
            pick = (wanted == id_row).astype(jnp.float32).astype(jnp.bfloat16)
            acc[pl.ds(at, row_block), :] += jnp.dot(
                pick, values, preferred_element_type=jnp.float32
            )
            return carry

        lax.fori_loop(0, share // row_block, rows, 0)

    run(groups, table_step)
    cent_copy.wait()

    def finish(m, carry):
        at = pl.ds(pl.multiple_of(m * row_block, row_block), row_block)
        updated = cent_buf[at, :].astype(jnp.float32) + acc[at, :]
        out_table[at, :] = normalised(updated).astype(jnp.bfloat16)
        return carry

    lax.fori_loop(0, share // row_block, finish, 0)

    def one_tile(i, carry):
        at = pl.ds(pl.multiple_of(i * tile, tile), tile)
        part = acc.at[pl.ds(0, tile)]
        part[...] = jnp.zeros((tile, acc.shape[1]), jnp.float32)
        groups = build(i + 1)

        def tile_step(id_row, values):
            pick = (own_ids[at, :] == id_row).astype(jnp.float32).astype(jnp.bfloat16)
            part[...] += jnp.dot(pick, values, preferred_element_type=jnp.float32)

        run(groups, tile_step)
        fresh = normalised(own_cent[at, :].astype(jnp.float32) + part[...]).astype(jnp.bfloat16)
        tile_res[at, :] = (own_emb[at, :].astype(jnp.float32) - fresh.astype(jnp.float32)).astype(
            jnp.bfloat16
        )
        return carry

    lax.fori_loop(0, tok // tile, one_tile, 0)

    def unsort(i, carry):
        at = pl.multiple_of(i * tile, tile)
        wanted = at + lax.broadcasted_iota(jnp.int32, (tile, tok), 0)
        pick = (wanted == order[...]).astype(jnp.float32).astype(jnp.bfloat16)
        out_res[pl.ds(at, tile), :] = jnp.dot(
            pick, tile_res[...], preferred_element_type=jnp.float32
        ).astype(jnp.bfloat16)
        return carry

    lax.fori_loop(0, tok // tile, unsort, 0)


def body(passages, cluster_ids, w_first, w_second, centroids):
    tok = passages.shape[0]
    owners = lax.axis_size(WIDE)
    reps = lax.axis_size("rep")
    blocks = owners * reps
    cent_rows, emb_width = centroids.shape
    share = cent_rows // reps
    capacity = 3 * tok // owners
    per_block = tok // CHUNK
    tile = min(256, tok)
    tiles = tok // tile
    wide_at = lax.axis_index(WIDE)
    rep_at = lax.axis_index("rep")

    sorted_ids, order = lax.sort((cluster_ids, lax.iota(jnp.int32, tok)), num_keys=1)

    hidden = jax.nn.gelu(
        jnp.dot(passages, w_first, preferred_element_type=jnp.float32), approximate=True
    ).astype(jnp.bfloat16)
    projected = jnp.dot(hidden, w_second, preferred_element_type=jnp.float32)
    embedded = normalised(projected).astype(jnp.bfloat16)
    to_sorted = (order[:, None] == jnp.arange(tok, dtype=jnp.int32)[None, :]).astype(jnp.bfloat16)
    own_emb = jnp.dot(to_sorted, embedded, preferred_element_type=jnp.float32).astype(jnp.bfloat16)
    id_bytes = jnp.stack([sorted_ids // 65536, sorted_ids // 256 % 256, sorted_ids % 256])
    id_part = id_bytes.astype(jnp.bfloat16).reshape(3 * tok // emb_width, emb_width)
    stride = tok + -(-id_part.shape[0] // 16) * 16
    outgoing = jnp.concatenate(
        [own_emb, jnp.pad(id_part, ((0, stride - tok - id_part.shape[0]), (0, 0)))]
    )
    same_core = lax.all_gather(outgoing, ("chip", "rep"), axis=0, tiled=True)
    all_emb = lax.all_gather(same_core, "core", axis=0, tiled=True)
    id_parts = all_emb.reshape(blocks, stride, emb_width)[:, tok : tok + id_part.shape[0]]
    id_parts = id_parts.astype(jnp.int32).reshape(blocks, 3, tok)
    all_ids = id_parts[:, 0] * 65536 + id_parts[:, 1] * 256 + id_parts[:, 2]

    owner_base = wide_at * cent_rows
    starts = jnp.sum(
        (sorted_ids[None, :] < jnp.arange(owners, dtype=jnp.int32)[:, None] * cent_rows).astype(
            jnp.int32
        ),
        axis=1,
    )
    ask_at = (starts[:, None] + jnp.arange(capacity, dtype=jnp.int32)[None, :]).reshape(-1)
    ask = jnp.sum(
        jnp.where(
            ask_at[:, None] == jnp.arange(tok, dtype=jnp.int32)[None, :], sorted_ids[None, :], 0
        ),
        axis=1,
    )
    asked = lax.all_to_all(ask, WIDE, split_axis=0, concat_axis=0, tiled=True)
    local = jnp.clip(asked - owner_base, 0, cent_rows - 1)
    picked = centroids[local]
    returned = lax.all_to_all(picked, WIDE, split_axis=0, concat_axis=0, tiled=True)
    owner_of = sorted_ids // cent_rows
    member = (owner_of[:, None] == jnp.arange(owners, dtype=jnp.int32)[None, :]).astype(jnp.int32)
    place = owner_of * capacity + lax.iota(jnp.int32, tok) - jnp.sum(member * starts[None, :], axis=1)
    own_cent = returned[place]

    share_base = owner_base + rep_at * share
    lows = jnp.concatenate([share_base[None], sorted_ids[::tile]])
    highs = jnp.concatenate([share_base[None] + share, sorted_ids[tile - 1 :: tile] + 1])
    first = jnp.sum((all_ids[None] < lows[:, None, None]).astype(jnp.int32), axis=2).reshape(-1)
    last = jnp.sum((all_ids[None] < highs[:, None, None]).astype(jnp.int32), axis=2).reshape(-1)
    scalars = jnp.stack([share_base, rep_at * share])
    id_rows = jnp.concatenate(
        [all_ids.reshape(blocks * per_block, CHUNK), jnp.full((8, CHUNK), -1, jnp.int32)]
    )

    resident = all_emb.size * 2 <= 24 * 1024 * 1024 and all_emb.shape[0] % (16 * GROUP) == 0
    held = all_emb.shape if resident else (2, GROUP * CHUNK, emb_width)
    smem = pl.BlockSpec(memory_space=pltpu.SMEM)
    vmem = pl.BlockSpec(memory_space=pltpu.VMEM)
    hbm = pl.BlockSpec(memory_space=pl.ANY)
    return pl.pallas_call(
        functools.partial(
            sums_kernel, blocks=blocks, per_block=per_block, stride=stride, tile=tile,
            row_block=min(512, share), resident=resident,
        ),
        out_shape=(
            jax.ShapeDtypeStruct((share, emb_width), jnp.bfloat16),
            jax.ShapeDtypeStruct((tok, emb_width), jnp.bfloat16),
        ),
        in_specs=[smem, smem, smem, hbm, vmem, hbm, vmem, vmem, vmem, vmem],
        out_specs=(vmem, vmem),
        scratch_shapes=[
            pltpu.SMEM((blocks * per_block + GROUP,), jnp.int32),
            pltpu.VMEM(held, jnp.bfloat16),
            pltpu.VMEM((share, emb_width), jnp.float32),
            pltpu.VMEM((share, emb_width), jnp.bfloat16),
            pltpu.VMEM((tok, emb_width), jnp.bfloat16),
            pltpu.SemaphoreType.DMA((2, GROUP)),
            pltpu.SemaphoreType.DMA,
        ],
        compiler_params=pltpu.CompilerParams(vmem_limit_bytes=48 * 1024 * 1024),
        cost_estimate=pl.CostEstimate(
            flops=30_000_000_000, bytes_accessed=40_000_000, transcendentals=0
        ),
    )(
        scalars, first, last, all_emb, id_rows, centroids, sorted_ids[:, None], own_cent, own_emb,
        order[None, :],
    )


def solution(mesh):
    wide, rep = mesh.devices.shape
    mesh = jax.sharding.Mesh(mesh.devices.reshape(wide // 2, 2, rep), ("chip", "core", "rep"))
    every = ("chip", "core", "rep")
    return jax.shard_map(
        body,
        mesh=mesh,
        in_specs=(P(every, None), P(every), P(), P(), P(WIDE, None)),
        out_specs=(P(every, None), P(every, None)),
        check_vma=False,
    )
```

```python
import functools

import jax
import jax.numpy as jnp
from jax import lax
from jax.experimental import pallas as pl
from jax.experimental.pallas import tpu as pltpu
from jax.sharding import PartitionSpec as P

CHUNK = 64
GROUP = 16
EPS = 1e-06
WIDE = "wide"


def normalised(values):
    return values * lax.rsqrt(jnp.mean(values * values, axis=-1, keepdims=True) + EPS)


def sums_kernel(
    scalars, first, last, emb, ids, cent, own_ids, own_cent, own_emb, order,
    out_table, out_res, chunks, slots, acc, cent_buf, tile_res, sems, cent_sem,
    *, blocks, per_block, stride, tile, row_block, resident,
):
    n_chunks = blocks * per_block
    share = out_table.shape[0]
    tok = own_ids.shape[0]
    wide = GROUP * CHUNK

    cent_copy = pltpu.make_async_copy(
        cent.at[pl.ds(pl.multiple_of(scalars[1], 16), share)], cent_buf, cent_sem
    )
    cent_copy.start()

    def row_of(n):
        return pl.multiple_of(lax.div(n, per_block) * stride + lax.rem(n, per_block) * CHUNK, 16)

    def whole_copies():
        rows = emb.shape[0] // 8
        return [
            pltpu.make_async_copy(
                emb.at[pl.ds(j * rows, rows)], slots.at[pl.ds(j * rows, rows)], sems.at[0, j]
            )
            for j in range(8)
        ]

    if resident:
        for copy in whole_copies():
            copy.start()

    def build(job):
        def block(k, count):
            begin = first[job * blocks + k]
            end = last[job * blocks + k]
            lo = begin // CHUNK
            hi = jnp.where(end > begin, (end + CHUNK - 1) // CHUNK, lo)

            def put(c, n):
                chunks[n] = k * per_block + c
                return n + 1

            return lax.fori_loop(lo, hi, put, count)

        count = lax.fori_loop(0, blocks, block, 0)
        for extra in range(GROUP):
            chunks[count + extra] = n_chunks
        return (count + GROUP - 1) // GROUP

    def copies(group, slot):
        made = []
        for j in range(GROUP):
            at = jnp.minimum(chunks[group * GROUP + j], n_chunks - 1)
            made.append(
                pltpu.make_async_copy(
                    emb.at[pl.ds(row_of(at), CHUNK)],
                    slots.at[slot, pl.ds(j * CHUNK, CHUNK)],
                    sems.at[slot, j],
                )
            )
        return made

    def id_row_of(group):
        row = [ids[pl.ds(chunks[group * GROUP + j], 1), :] for j in range(GROUP)]
        return jnp.concatenate(row, axis=1)

    def run_resident(groups, step):
        def body(group, carry):
            at = [jnp.minimum(chunks[group * GROUP + j], n_chunks - 1) for j in range(GROUP)]
            rows = jnp.concatenate([slots[pl.ds(row_of(n), CHUNK), :] for n in at], axis=0)
            step(id_row_of(group), rows)
            return carry

        lax.fori_loop(0, groups, body, 0)

    def run_streamed(groups, step):
        @pl.when(groups > 0)
        def _():
            for copy in copies(0, 0):
                copy.start()

        def body(group, carry):
            slot = lax.rem(group, 2)

            @pl.when(group + 1 < groups)
            def _():
                for copy in copies(group + 1, 1 - slot):
                    copy.start()

            for copy in copies(group, slot):
                copy.wait()
            step(id_row_of(group), slots[slot])
            return carry

        lax.fori_loop(0, groups, body, 0)

    run = run_resident if resident else run_streamed

    acc[...] = jnp.zeros_like(acc)
    groups = build(0)
    if resident:
        for copy in whole_copies():
            copy.wait()

    def table_step(id_row, values):
        def rows(m, carry):
            at = pl.multiple_of(m * row_block, row_block)
            wanted = scalars[0] + at + lax.broadcasted_iota(jnp.int32, (row_block, wide), 0)
            pick = (wanted == id_row).astype(jnp.float32).astype(jnp.bfloat16)
            acc[pl.ds(at, row_block), :] += jnp.dot(
                pick, values, preferred_element_type=jnp.float32
            )
            return carry

        lax.fori_loop(0, share // row_block, rows, 0)

    run(groups, table_step)
    cent_copy.wait()

    def finish(m, carry):
        at = pl.ds(pl.multiple_of(m * row_block, row_block), row_block)
        updated = cent_buf[at, :].astype(jnp.float32) + acc[at, :]
        out_table[at, :] = normalised(updated).astype(jnp.bfloat16)
        return carry

    lax.fori_loop(0, share // row_block, finish, 0)

    def one_tile(i, carry):
        at = pl.ds(pl.multiple_of(i * tile, tile), tile)
        part = acc.at[pl.ds(0, tile)]
        part[...] = jnp.zeros((tile, acc.shape[1]), jnp.float32)
        groups = build(i + 1)

        def tile_step(id_row, values):
            pick = (own_ids[at, :] == id_row).astype(jnp.float32).astype(jnp.bfloat16)
            part[...] += jnp.dot(pick, values, preferred_element_type=jnp.float32)

        run(groups, tile_step)
        fresh = normalised(own_cent[at, :].astype(jnp.float32) + part[...]).astype(jnp.bfloat16)
        tile_res[at, :] = (own_emb[at, :].astype(jnp.float32) - fresh.astype(jnp.float32)).astype(
            jnp.bfloat16
        )
        return carry

    lax.fori_loop(0, tok // tile, one_tile, 0)

    def unsort(i, carry):
        at = pl.multiple_of(i * tile, tile)
        wanted = at + lax.broadcasted_iota(jnp.int32, (tile, tok), 0)
        pick = (wanted == order[...]).astype(jnp.float32).astype(jnp.bfloat16)
        out_res[pl.ds(at, tile), :] = jnp.dot(
            pick, tile_res[...], preferred_element_type=jnp.float32
        ).astype(jnp.bfloat16)
        return carry

    lax.fori_loop(0, tok // tile, unsort, 0)


def body(passages, cluster_ids, w_first, w_second, centroids):
    tok = passages.shape[0]
    owners = lax.axis_size(WIDE)
    reps = lax.axis_size("rep")
    blocks = owners * reps
    cent_rows, emb_width = centroids.shape
    share = cent_rows // reps
    capacity = 3 * tok // owners
    per_block = tok // CHUNK
    tile = min(256, tok)
    tiles = tok // tile
    wide_at = lax.axis_index(WIDE)
    rep_at = lax.axis_index("rep")

    sorted_ids, order = lax.sort((cluster_ids, lax.iota(jnp.int32, tok)), num_keys=1)

    hidden = jax.nn.gelu(
        jnp.dot(passages, w_first, preferred_element_type=jnp.float32), approximate=True
    ).astype(jnp.bfloat16)
    projected = jnp.dot(hidden, w_second, preferred_element_type=jnp.float32)
    embedded = normalised(projected).astype(jnp.bfloat16)
    to_sorted = (order[:, None] == jnp.arange(tok, dtype=jnp.int32)[None, :]).astype(jnp.bfloat16)
    own_emb = jnp.dot(to_sorted, embedded, preferred_element_type=jnp.float32).astype(jnp.bfloat16)
    id_bytes = jnp.stack([sorted_ids // 65536, sorted_ids // 256 % 256, sorted_ids % 256])
    id_part = id_bytes.astype(jnp.bfloat16).reshape(3 * tok // emb_width, emb_width)
    stride = tok + -(-id_part.shape[0] // 16) * 16
    outgoing = jnp.concatenate(
        [own_emb, jnp.pad(id_part, ((0, stride - tok - id_part.shape[0]), (0, 0)))]
    )
    all_emb = lax.all_gather(outgoing, ("wide", "rep"), axis=0, tiled=True)
    id_parts = all_emb.reshape(blocks, stride, emb_width)[:, tok : tok + id_part.shape[0]]
    id_parts = id_parts.astype(jnp.int32).reshape(blocks, 3, tok)
    all_ids = id_parts[:, 0] * 65536 + id_parts[:, 1] * 256 + id_parts[:, 2]

    owner_base = wide_at * cent_rows
    starts = jnp.sum(
        (sorted_ids[None, :] < jnp.arange(owners, dtype=jnp.int32)[:, None] * cent_rows).astype(
            jnp.int32
        ),
        axis=1,
    )
    ask_at = (starts[:, None] + jnp.arange(capacity, dtype=jnp.int32)[None, :]).reshape(-1)
    ask = jnp.sum(
        jnp.where(
            ask_at[:, None] == jnp.arange(tok, dtype=jnp.int32)[None, :], sorted_ids[None, :], 0
        ),
        axis=1,
    )
    asked = lax.all_to_all(ask, WIDE, split_axis=0, concat_axis=0, tiled=True)
    local = jnp.clip(asked - owner_base, 0, cent_rows - 1)
    picked = centroids[local]
    returned = lax.all_to_all(picked, WIDE, split_axis=0, concat_axis=0, tiled=True)
    owner_of = sorted_ids // cent_rows
    member = (owner_of[:, None] == jnp.arange(owners, dtype=jnp.int32)[None, :]).astype(jnp.int32)
    place = owner_of * capacity + lax.iota(jnp.int32, tok) - jnp.sum(member * starts[None, :], axis=1)
    own_cent = returned[place]

    share_base = owner_base + rep_at * share
    lows = jnp.concatenate([share_base[None], sorted_ids[::tile]])
    highs = jnp.concatenate([share_base[None] + share, sorted_ids[tile - 1 :: tile] + 1])
    first = jnp.sum((all_ids[None] < lows[:, None, None]).astype(jnp.int32), axis=2).reshape(-1)
    last = jnp.sum((all_ids[None] < highs[:, None, None]).astype(jnp.int32), axis=2).reshape(-1)
    scalars = jnp.stack([share_base, rep_at * share])
    id_rows = jnp.concatenate(
        [all_ids.reshape(blocks * per_block, CHUNK), jnp.full((8, CHUNK), -1, jnp.int32)]
    )

    resident = all_emb.size * 2 <= 24 * 1024 * 1024 and all_emb.shape[0] % 128 == 0
    held = all_emb.shape if resident else (2, GROUP * CHUNK, emb_width)
    smem = pl.BlockSpec(memory_space=pltpu.SMEM)
    vmem = pl.BlockSpec(memory_space=pltpu.VMEM)
    hbm = pl.BlockSpec(memory_space=pl.ANY)
    return pl.pallas_call(
        functools.partial(
            sums_kernel, blocks=blocks, per_block=per_block, stride=stride, tile=tile,
            row_block=min(512, share), resident=resident,
        ),
        out_shape=(
            jax.ShapeDtypeStruct((share, emb_width), jnp.bfloat16),
            jax.ShapeDtypeStruct((tok, emb_width), jnp.bfloat16),
        ),
        in_specs=[smem, smem, smem, hbm, vmem, hbm, vmem, vmem, vmem, vmem],
        out_specs=(vmem, vmem),
        scratch_shapes=[
            pltpu.SMEM((blocks * per_block + GROUP,), jnp.int32),
            pltpu.VMEM(held, jnp.bfloat16),
            pltpu.VMEM((share, emb_width), jnp.float32),
            pltpu.VMEM((share, emb_width), jnp.bfloat16),
            pltpu.VMEM((tok, emb_width), jnp.bfloat16),
            pltpu.SemaphoreType.DMA((2, GROUP)),
            pltpu.SemaphoreType.DMA,
        ],
        compiler_params=pltpu.CompilerParams(vmem_limit_bytes=48 * 1024 * 1024),
        cost_estimate=pl.CostEstimate(
            flops=30_000_000_000, bytes_accessed=40_000_000, transcendentals=0
        ),
    )(
        scalars, first, last, all_emb, id_rows, centroids, sorted_ids[:, None], own_cent, own_emb,
        order[None, :],
    )


def solution(mesh):
    return jax.shard_map(
        body,
        mesh=mesh,
        in_specs=(P(("wide", "rep"), None), P(("wide", "rep")), P(), P(), P("wide", None)),
        out_specs=(P(("wide", "rep"), None), P(("wide", "rep"), None)),
        check_vma=False,
    )
```

```python
import functools

import jax
import jax.numpy as jnp
from jax import lax
from jax.experimental import pallas as pl
from jax.experimental.pallas import tpu as pltpu
from jax.sharding import PartitionSpec as P

CHUNK = 64
GROUP = 16
EPS = 1e-06
WIDE = "wide"


def normalised(values):
    return values * lax.rsqrt(jnp.mean(values * values, axis=-1, keepdims=True) + EPS)


def sums_kernel(
    scalars, first, last, emb, ids, cent, own_ids, own_cent, own_emb, order,
    out_table, out_res, chunks, slots, acc, cent_buf, tile_res, sems, cent_sem,
    *, blocks, per_block, stride, tile, row_block, resident,
):
    n_chunks = blocks * per_block
    share = out_table.shape[0]
    tok = own_ids.shape[0]
    wide = GROUP * CHUNK

    cent_copy = pltpu.make_async_copy(
        cent.at[pl.ds(pl.multiple_of(scalars[1], 16), share)], cent_buf, cent_sem
    )
    cent_copy.start()

    def row_of(n):
        return pl.multiple_of(lax.div(n, per_block) * stride + lax.rem(n, per_block) * CHUNK, 16)

    def whole_copies():
        rows = emb.shape[0] // 8
        return [
            pltpu.make_async_copy(
                emb.at[pl.ds(j * rows, rows)], slots.at[pl.ds(j * rows, rows)], sems.at[0, j]
            )
            for j in range(8)
        ]

    if resident:
        for copy in whole_copies():
            copy.start()

    def build(job):
        def block(k, count):
            begin = first[job * blocks + k]
            end = last[job * blocks + k]
            lo = begin // CHUNK
            hi = jnp.where(end > begin, (end + CHUNK - 1) // CHUNK, lo)

            def put(c, n):
                chunks[n] = k * per_block + c
                return n + 1

            return lax.fori_loop(lo, hi, put, count)

        count = lax.fori_loop(0, blocks, block, 0)
        for extra in range(GROUP):
            chunks[count + extra] = n_chunks
        return (count + GROUP - 1) // GROUP

    def copies(group, slot):
        made = []
        for j in range(GROUP):
            at = jnp.minimum(chunks[group * GROUP + j], n_chunks - 1)
            made.append(
                pltpu.make_async_copy(
                    emb.at[pl.ds(row_of(at), CHUNK)],
                    slots.at[slot, pl.ds(j * CHUNK, CHUNK)],
                    sems.at[slot, j],
                )
            )
        return made

    def id_row_of(group):
        row = [ids[pl.ds(chunks[group * GROUP + j], 1), :] for j in range(GROUP)]
        return jnp.concatenate(row, axis=1)

    def run_resident(groups, step):
        def body(group, carry):
            at = [jnp.minimum(chunks[group * GROUP + j], n_chunks - 1) for j in range(GROUP)]
            rows = jnp.concatenate([slots[pl.ds(row_of(n), CHUNK), :] for n in at], axis=0)
            step(id_row_of(group), rows)
            return carry

        lax.fori_loop(0, groups, body, 0)

    def run_streamed(groups, step):
        @pl.when(groups > 0)
        def _():
            for copy in copies(0, 0):
                copy.start()

        def body(group, carry):
            slot = lax.rem(group, 2)

            @pl.when(group + 1 < groups)
            def _():
                for copy in copies(group + 1, 1 - slot):
                    copy.start()

            for copy in copies(group, slot):
                copy.wait()
            step(id_row_of(group), slots[slot])
            return carry

        lax.fori_loop(0, groups, body, 0)

    run = run_resident if resident else run_streamed

    acc[...] = jnp.zeros_like(acc)
    groups = build(0)
    if resident:
        for copy in whole_copies():
            copy.wait()

    wanted = lax.broadcasted_iota(jnp.int32, (row_block, wide), 0).astype(jnp.int16)

    def table_step(id_row, values):
        def rows(m, carry):
            at = pl.multiple_of(m * row_block, row_block)
            local = jnp.clip(id_row - (scalars[0] + at), -1, row_block).astype(jnp.int16)
            pick = jnp.where(wanted == local, jnp.bfloat16(1), jnp.bfloat16(0))
            acc[pl.ds(at, row_block), :] += jnp.dot(
                pick, values, preferred_element_type=jnp.float32
            )
            return carry

        lax.fori_loop(0, share // row_block, rows, 0)

    run(groups, table_step)
    cent_copy.wait()

    def finish(m, carry):
        at = pl.ds(pl.multiple_of(m * row_block, row_block), row_block)
        updated = cent_buf[at, :].astype(jnp.float32) + acc[at, :]
        out_table[at, :] = normalised(updated).astype(jnp.bfloat16)
        return carry

    lax.fori_loop(0, share // row_block, finish, 0)

    def one_tile(i, carry):
        at = pl.ds(pl.multiple_of(i * tile, tile), tile)
        part = acc.at[pl.ds(0, tile)]
        part[...] = jnp.zeros((tile, acc.shape[1]), jnp.float32)
        groups = build(i + 1)

        def tile_step(id_row, values):
            pick = (own_ids[at, :] == id_row).astype(jnp.float32).astype(jnp.bfloat16)
            part[...] += jnp.dot(pick, values, preferred_element_type=jnp.float32)

        run(groups, tile_step)
        fresh = normalised(own_cent[at, :].astype(jnp.float32) + part[...]).astype(jnp.bfloat16)
        tile_res[at, :] = (own_emb[at, :].astype(jnp.float32) - fresh.astype(jnp.float32)).astype(
            jnp.bfloat16
        )
        return carry

    lax.fori_loop(0, tok // tile, one_tile, 0)

    def unsort(i, carry):
        at = pl.multiple_of(i * tile, tile)
        wanted = at + lax.broadcasted_iota(jnp.int32, (tile, tok), 0)
        pick = (wanted == order[...]).astype(jnp.float32).astype(jnp.bfloat16)
        out_res[pl.ds(at, tile), :] = jnp.dot(
            pick, tile_res[...], preferred_element_type=jnp.float32
        ).astype(jnp.bfloat16)
        return carry

    lax.fori_loop(0, tok // tile, unsort, 0)


def body(passages, cluster_ids, w_first, w_second, centroids):
    tok = passages.shape[0]
    owners = lax.axis_size(WIDE)
    reps = lax.axis_size("rep")
    blocks = owners * reps
    cent_rows, emb_width = centroids.shape
    share = cent_rows // reps
    capacity = 3 * tok // owners
    per_block = tok // CHUNK
    tile = min(256, tok)
    tiles = tok // tile
    wide_at = lax.axis_index(WIDE)
    rep_at = lax.axis_index("rep")

    sorted_ids, order = lax.sort((cluster_ids, lax.iota(jnp.int32, tok)), num_keys=1)

    hidden = jax.nn.gelu(
        jnp.dot(passages, w_first, preferred_element_type=jnp.float32), approximate=True
    ).astype(jnp.bfloat16)
    projected = jnp.dot(hidden, w_second, preferred_element_type=jnp.float32)
    embedded = normalised(projected).astype(jnp.bfloat16)
    to_sorted = (order[:, None] == jnp.arange(tok, dtype=jnp.int32)[None, :]).astype(jnp.bfloat16)
    own_emb = jnp.dot(to_sorted, embedded, preferred_element_type=jnp.float32).astype(jnp.bfloat16)
    id_bytes = jnp.stack([sorted_ids // 65536, sorted_ids // 256 % 256, sorted_ids % 256])
    id_part = id_bytes.astype(jnp.bfloat16).reshape(3 * tok // emb_width, emb_width)
    stride = tok + -(-id_part.shape[0] // 16) * 16
    outgoing = jnp.concatenate(
        [own_emb, jnp.pad(id_part, ((0, stride - tok - id_part.shape[0]), (0, 0)))]
    )
    all_emb = lax.all_gather(outgoing, ("wide", "rep"), axis=0, tiled=True)
    id_parts = all_emb.reshape(blocks, stride, emb_width)[:, tok : tok + id_part.shape[0]]
    id_parts = id_parts.astype(jnp.int32).reshape(blocks, 3, tok)
    all_ids = id_parts[:, 0] * 65536 + id_parts[:, 1] * 256 + id_parts[:, 2]

    owner_base = wide_at * cent_rows
    starts = jnp.sum(
        (sorted_ids[None, :] < jnp.arange(owners, dtype=jnp.int32)[:, None] * cent_rows).astype(
            jnp.int32
        ),
        axis=1,
    )
    ask_at = (starts[:, None] + jnp.arange(capacity, dtype=jnp.int32)[None, :]).reshape(-1)
    ask = jnp.sum(
        jnp.where(
            ask_at[:, None] == jnp.arange(tok, dtype=jnp.int32)[None, :], sorted_ids[None, :], 0
        ),
        axis=1,
    )
    asked = lax.all_to_all(ask, WIDE, split_axis=0, concat_axis=0, tiled=True)
    local = jnp.clip(asked - owner_base, 0, cent_rows - 1)
    picked = centroids[local]
    returned = lax.all_to_all(picked, WIDE, split_axis=0, concat_axis=0, tiled=True)
    owner_of = sorted_ids // cent_rows
    member = (owner_of[:, None] == jnp.arange(owners, dtype=jnp.int32)[None, :]).astype(jnp.int32)
    place = owner_of * capacity + lax.iota(jnp.int32, tok) - jnp.sum(member * starts[None, :], axis=1)
    own_cent = returned[place]

    share_base = owner_base + rep_at * share
    lows = jnp.concatenate([share_base[None], sorted_ids[::tile]])
    highs = jnp.concatenate([share_base[None] + share, sorted_ids[tile - 1 :: tile] + 1])
    first = jnp.sum((all_ids[None] < lows[:, None, None]).astype(jnp.int32), axis=2).reshape(-1)
    last = jnp.sum((all_ids[None] < highs[:, None, None]).astype(jnp.int32), axis=2).reshape(-1)
    scalars = jnp.stack([share_base, rep_at * share])
    id_rows = jnp.concatenate(
        [all_ids.reshape(blocks * per_block, CHUNK), jnp.full((8, CHUNK), -1, jnp.int32)]
    )

    resident = all_emb.size * 2 <= 24 * 1024 * 1024 and all_emb.shape[0] % 128 == 0
    held = all_emb.shape if resident else (2, GROUP * CHUNK, emb_width)
    smem = pl.BlockSpec(memory_space=pltpu.SMEM)
    vmem = pl.BlockSpec(memory_space=pltpu.VMEM)
    hbm = pl.BlockSpec(memory_space=pl.ANY)
    return pl.pallas_call(
        functools.partial(
            sums_kernel, blocks=blocks, per_block=per_block, stride=stride, tile=tile,
            row_block=min(512, share), resident=resident,
        ),
        out_shape=(
            jax.ShapeDtypeStruct((share, emb_width), jnp.bfloat16),
            jax.ShapeDtypeStruct((tok, emb_width), jnp.bfloat16),
        ),
        in_specs=[smem, smem, smem, hbm, vmem, hbm, vmem, vmem, vmem, vmem],
        out_specs=(vmem, vmem),
        scratch_shapes=[
            pltpu.SMEM((blocks * per_block + GROUP,), jnp.int32),
            pltpu.VMEM(held, jnp.bfloat16),
            pltpu.VMEM((share, emb_width), jnp.float32),
            pltpu.VMEM((share, emb_width), jnp.bfloat16),
            pltpu.VMEM((tok, emb_width), jnp.bfloat16),
            pltpu.SemaphoreType.DMA((2, GROUP)),
            pltpu.SemaphoreType.DMA,
        ],
        compiler_params=pltpu.CompilerParams(vmem_limit_bytes=48 * 1024 * 1024),
        cost_estimate=pl.CostEstimate(
            flops=30_000_000_000, bytes_accessed=40_000_000, transcendentals=0
        ),
    )(
        scalars, first, last, all_emb, id_rows, centroids, sorted_ids[:, None], own_cent, own_emb,
        order[None, :],
    )


def solution(mesh):
    return jax.shard_map(
        body,
        mesh=mesh,
        in_specs=(P(("wide", "rep"), None), P(("wide", "rep")), P(), P(), P("wide", None)),
        out_specs=(P(("wide", "rep"), None), P(("wide", "rep"), None)),
        check_vma=False,
    )
```

```python
import functools

import jax
import jax.numpy as jnp
from jax import lax
from jax.experimental import pallas as pl
from jax.experimental.pallas import tpu as pltpu
from jax.sharding import PartitionSpec as P

CHUNK = 64
GROUP = 16
EPS = 1e-06
WIDE = "wide"


def normalised(values):
    return values * lax.rsqrt(jnp.mean(values * values, axis=-1, keepdims=True) + EPS)


def sums_kernel(
    scalars, first, last, emb, ids, cent, own_ids, own_cent, own_emb, order,
    out_table, out_res, chunks, slots, acc, cent_buf, tile_res, sems, cent_sem,
    *, blocks, per_block, stride, tile, row_block, resident,
):
    n_chunks = blocks * per_block
    share = out_table.shape[0]
    tok = own_ids.shape[0]
    wide = GROUP * CHUNK

    cent_copy = pltpu.make_async_copy(
        cent.at[pl.ds(pl.multiple_of(scalars[1], 16), share)], cent_buf, cent_sem
    )
    cent_copy.start()

    def row_of(n):
        return pl.multiple_of(lax.div(n, per_block) * stride + lax.rem(n, per_block) * CHUNK, 16)

    def whole_copies():
        rows = emb.shape[0] // 8
        return [
            pltpu.make_async_copy(
                emb.at[pl.ds(j * rows, rows)], slots.at[pl.ds(j * rows, rows)], sems.at[0, j]
            )
            for j in range(8)
        ]

    if resident:
        for copy in whole_copies():
            copy.start()

    def build(job):
        def block(k, count):
            begin = first[job * blocks + k]
            end = last[job * blocks + k]
            lo = begin // CHUNK
            hi = jnp.where(end > begin, (end + CHUNK - 1) // CHUNK, lo)

            def put(c, n):
                chunks[n] = k * per_block + c
                return n + 1

            return lax.fori_loop(lo, hi, put, count)

        count = lax.fori_loop(0, blocks, block, 0)
        for extra in range(GROUP):
            chunks[count + extra] = n_chunks
        return (count + GROUP - 1) // GROUP

    def copies(group, slot):
        made = []
        for j in range(GROUP):
            at = jnp.minimum(chunks[group * GROUP + j], n_chunks - 1)
            made.append(
                pltpu.make_async_copy(
                    emb.at[pl.ds(row_of(at), CHUNK)],
                    slots.at[slot, pl.ds(j * CHUNK, CHUNK)],
                    sems.at[slot, j],
                )
            )
        return made

    def id_row_of(group):
        row = [ids[pl.ds(chunks[group * GROUP + j], 1), :] for j in range(GROUP)]
        return jnp.concatenate(row, axis=1)

    def run_resident(groups, step):
        def body(group, carry):
            at = [jnp.minimum(chunks[group * GROUP + j], n_chunks - 1) for j in range(GROUP)]
            rows = jnp.concatenate([slots[pl.ds(row_of(n), CHUNK), :] for n in at], axis=0)
            step(id_row_of(group), rows)
            return carry

        lax.fori_loop(0, groups, body, 0)

    def run_streamed(groups, step):
        @pl.when(groups > 0)
        def _():
            for copy in copies(0, 0):
                copy.start()

        def body(group, carry):
            slot = lax.rem(group, 2)

            @pl.when(group + 1 < groups)
            def _():
                for copy in copies(group + 1, 1 - slot):
                    copy.start()

            for copy in copies(group, slot):
                copy.wait()
            step(id_row_of(group), slots[slot])
            return carry

        lax.fori_loop(0, groups, body, 0)

    run = run_resident if resident else run_streamed

    acc[...] = jnp.zeros_like(acc)
    groups = build(0)
    if resident:
        for copy in whole_copies():
            copy.wait()

    wanted = lax.broadcasted_iota(jnp.int32, (row_block, wide), 0).astype(jnp.int16)

    def table_step(id_row, values):
        def rows(m, carry):
            at = pl.multiple_of(m * row_block, row_block)
            local = jnp.clip(id_row - (scalars[0] + at), -1, row_block).astype(jnp.int16)
            pick = jnp.where(wanted == local, jnp.bfloat16(1), jnp.bfloat16(0))
            acc[pl.ds(at, row_block), :] += jnp.dot(
                pick, values, preferred_element_type=jnp.float32
            )
            return carry

        lax.fori_loop(0, share // row_block, rows, 0)

    run(groups, table_step)
    cent_copy.wait()

    def finish(m, carry):
        at = pl.ds(pl.multiple_of(m * row_block, row_block), row_block)
        updated = cent_buf[at, :].astype(jnp.float32) + acc[at, :]
        out_table[at, :] = normalised(updated).astype(jnp.bfloat16)
        return carry

    lax.fori_loop(0, share // row_block, finish, 0)

    def one_tile(i, carry):
        at = pl.ds(pl.multiple_of(i * tile, tile), tile)
        part = acc.at[pl.ds(0, tile)]
        part[...] = jnp.zeros((tile, acc.shape[1]), jnp.float32)
        groups = build(i + 1)

        def tile_step(id_row, values):
            pick = (own_ids[at, :] == id_row).astype(jnp.float32).astype(jnp.bfloat16)
            part[...] += jnp.dot(pick, values, preferred_element_type=jnp.float32)

        run(groups, tile_step)
        fresh = normalised(own_cent[at, :].astype(jnp.float32) + part[...]).astype(jnp.bfloat16)
        tile_res[at, :] = (own_emb[at, :].astype(jnp.float32) - fresh.astype(jnp.float32)).astype(
            jnp.bfloat16
        )
        return carry

    lax.fori_loop(0, tok // tile, one_tile, 0)

    def unsort(i, carry):
        at = pl.multiple_of(i * tile, tile)
        wanted = at + lax.broadcasted_iota(jnp.int32, (tile, tok), 0)
        pick = (wanted == order[...]).astype(jnp.float32).astype(jnp.bfloat16)
        out_res[pl.ds(at, tile), :] = jnp.dot(
            pick, tile_res[...], preferred_element_type=jnp.float32
        ).astype(jnp.bfloat16)
        return carry

    lax.fori_loop(0, tok // tile, unsort, 0)


def body(passages, cluster_ids, w_first, w_second, centroids):
    tok = passages.shape[0]
    owners = lax.axis_size(WIDE)
    reps = lax.axis_size("rep")
    blocks = owners * reps
    cent_rows, emb_width = centroids.shape
    share = cent_rows // reps
    capacity = 3 * tok // owners
    per_block = tok // CHUNK
    tile = min(256, tok)
    tiles = tok // tile
    wide_at = lax.axis_index(WIDE)
    rep_at = lax.axis_index("rep")

    at = lax.iota(jnp.int32, tok)
    ahead = (cluster_ids[None, :] < cluster_ids[:, None]) | (
        (cluster_ids[None, :] == cluster_ids[:, None]) & (at[None, :] < at[:, None])
    )
    rank = jnp.sum(ahead.astype(jnp.int32), axis=1)
    here = rank[None, :] == at[:, None]
    sorted_ids = jnp.sum(jnp.where(here, cluster_ids[None, :], 0), axis=1)
    order = jnp.sum(jnp.where(here, at[None, :], 0), axis=1)

    hidden = jax.nn.gelu(
        jnp.dot(passages, w_first, preferred_element_type=jnp.float32), approximate=True
    ).astype(jnp.bfloat16)
    projected = jnp.dot(hidden, w_second, preferred_element_type=jnp.float32)
    embedded = normalised(projected).astype(jnp.bfloat16)
    to_sorted = here.astype(jnp.bfloat16)
    own_emb = jnp.dot(to_sorted, embedded, preferred_element_type=jnp.float32).astype(jnp.bfloat16)
    id_bytes = jnp.stack([sorted_ids // 65536, sorted_ids // 256 % 256, sorted_ids % 256])
    id_part = id_bytes.astype(jnp.bfloat16).reshape(3 * tok // emb_width, emb_width)
    stride = tok + -(-id_part.shape[0] // 16) * 16
    outgoing = jnp.concatenate(
        [own_emb, jnp.pad(id_part, ((0, stride - tok - id_part.shape[0]), (0, 0)))]
    )
    all_emb = lax.all_gather(outgoing, ("wide", "rep"), axis=0, tiled=True)
    id_parts = all_emb.reshape(blocks, stride, emb_width)[:, tok : tok + id_part.shape[0]]
    id_parts = id_parts.astype(jnp.int32).reshape(blocks, 3, tok)
    all_ids = id_parts[:, 0] * 65536 + id_parts[:, 1] * 256 + id_parts[:, 2]

    owner_base = wide_at * cent_rows
    starts = jnp.sum(
        (sorted_ids[None, :] < jnp.arange(owners, dtype=jnp.int32)[:, None] * cent_rows).astype(
            jnp.int32
        ),
        axis=1,
    )
    ask_at = (starts[:, None] + jnp.arange(capacity, dtype=jnp.int32)[None, :]).reshape(-1)
    ask = jnp.sum(
        jnp.where(
            ask_at[:, None] == jnp.arange(tok, dtype=jnp.int32)[None, :], sorted_ids[None, :], 0
        ),
        axis=1,
    )
    asked = lax.all_to_all(ask, WIDE, split_axis=0, concat_axis=0, tiled=True)
    local = jnp.clip(asked - owner_base, 0, cent_rows - 1)
    picked = centroids[local]
    returned = lax.all_to_all(picked, WIDE, split_axis=0, concat_axis=0, tiled=True)
    owner_of = sorted_ids // cent_rows
    member = (owner_of[:, None] == jnp.arange(owners, dtype=jnp.int32)[None, :]).astype(jnp.int32)
    place = owner_of * capacity + lax.iota(jnp.int32, tok) - jnp.sum(member * starts[None, :], axis=1)
    own_cent = returned[place]

    share_base = owner_base + rep_at * share
    lows = jnp.concatenate([share_base[None], sorted_ids[::tile]])
    highs = jnp.concatenate([share_base[None] + share, sorted_ids[tile - 1 :: tile] + 1])
    first = jnp.sum((all_ids[None] < lows[:, None, None]).astype(jnp.int32), axis=2).reshape(-1)
    last = jnp.sum((all_ids[None] < highs[:, None, None]).astype(jnp.int32), axis=2).reshape(-1)
    scalars = jnp.stack([share_base, rep_at * share])
    id_rows = jnp.concatenate(
        [all_ids.reshape(blocks * per_block, CHUNK), jnp.full((8, CHUNK), -1, jnp.int32)]
    )

    resident = all_emb.size * 2 <= 24 * 1024 * 1024 and all_emb.shape[0] % 128 == 0
    held = all_emb.shape if resident else (2, GROUP * CHUNK, emb_width)
    smem = pl.BlockSpec(memory_space=pltpu.SMEM)
    vmem = pl.BlockSpec(memory_space=pltpu.VMEM)
    hbm = pl.BlockSpec(memory_space=pl.ANY)
    return pl.pallas_call(
        functools.partial(
            sums_kernel, blocks=blocks, per_block=per_block, stride=stride, tile=tile,
            row_block=min(512, share), resident=resident,
        ),
        out_shape=(
            jax.ShapeDtypeStruct((share, emb_width), jnp.bfloat16),
            jax.ShapeDtypeStruct((tok, emb_width), jnp.bfloat16),
        ),
        in_specs=[smem, smem, smem, hbm, vmem, hbm, vmem, vmem, vmem, vmem],
        out_specs=(vmem, vmem),
        scratch_shapes=[
            pltpu.SMEM((blocks * per_block + GROUP,), jnp.int32),
            pltpu.VMEM(held, jnp.bfloat16),
            pltpu.VMEM((share, emb_width), jnp.float32),
            pltpu.VMEM((share, emb_width), jnp.bfloat16),
            pltpu.VMEM((tok, emb_width), jnp.bfloat16),
            pltpu.SemaphoreType.DMA((2, GROUP)),
            pltpu.SemaphoreType.DMA,
        ],
        compiler_params=pltpu.CompilerParams(vmem_limit_bytes=48 * 1024 * 1024),
        cost_estimate=pl.CostEstimate(
            flops=30_000_000_000, bytes_accessed=40_000_000, transcendentals=0
        ),
    )(
        scalars, first, last, all_emb, id_rows, centroids, sorted_ids[:, None], own_cent, own_emb,
        order[None, :],
    )


def solution(mesh):
    return jax.shard_map(
        body,
        mesh=mesh,
        in_specs=(P(("wide", "rep"), None), P(("wide", "rep")), P(), P(), P("wide", None)),
        out_specs=(P(("wide", "rep"), None), P(("wide", "rep"), None)),
        check_vma=False,
    )
```
